1024 devices in a mesh: replica: 16 (over x_hi, z), expert: 32 (over y, x_lo), tensor: 2 (over core).
Axes of the slice: x: 8 (x_hi: 2, x_lo: 4; x = x_hi * 4 + x_lo), y: 8, z: 8, core: 2. Of those that a mesh axis runs over, the one named last changes fastest.
Arguments:
- queries: bfloat16 [4, 512, 128, 576], P(None, ('replica', 'expert'), 'tensor'), may hold values from -276 to 276
- latent_cache: bfloat16 [512, 1024, 576], P(('replica', 'expert')), may hold values from -6 to 6
- cache_lengths: int32 [512], P(('replica', 'expert')), may hold values from 1 to 1020, 261120 in all
- hidden_acts: bfloat16 [8192, 2, 2048], P(('replica', 'expert')), may hold values from -6 to 6
- routes: int32 [8192, 2], P(('replica', 'expert')), may hold values from 0 to 31, all different within a row; in each aligned block of 16 rows (0 to 15, 16 to 31, ...) at most 2 rows name the same one
- route_weights: float32 [8192, 2], P(('replica', 'expert')), may hold values from 0.2 to 1
- stored_values: bfloat16 [32, 2048, 7168], P('expert', ('replica', 'tensor')), may hold values from -0.125 to 0.125
- block_scales: float32 [32, 16, 56], P('expert'), may hold values from 0.25 to 4
Outputs:
- attended: bfloat16 [4, 512, 128, 512], P(None, ('replica', 'expert'), 'tensor')
- synced_weights: bfloat16 [32, 2048, 7168], P('expert', None, ('replica', 'tensor'))
- expert_output: bfloat16 [8192, 16, 2, 224], P(('replica', 'expert'), None, 'tensor')
The draws below stay inside these ranges and needn't reach their ends.
Inputs may be any that keep to these rules, and one draw needn't show every extreme that they name: `routes`: A row names 2 different experts, and no expert is named by more than 2 of the 16 rows of one device. `cache_lengths`: each sequence leaves room for the 4 new tokens; the lengths sum to 261120.
All inputs are finite; a program needn't handle non-finite values. No bound on the sum of `cache_lengths` on one device may be relied on, other than what follows from the above.
Results may differ from the reference program's by a relative error of at most 0.0057.
Values may be sent and summed in bfloat16 or wider, within the bound.
A program may use at most 64 MiB of HBM per device.

```python
import math
import jax
import jax.numpy as jnp
import numpy as np
from jax import lax

D = 7168
FFN = 2048
HEADS = 128
LATENT = 512
ROPE = 64
QB = 128
STEPS = 4
L = 1024
TOK_DEV = 16
TOP_F = 2
EXPERTS_F = 32
MOST = 2
SEQS = 512
TOKENS = 8192
DB = 224
N_REPLICA = 16
N_EXPERT = 32
N_TENSOR = 2


def draw_latent_cache(key, part):
    key = jax.random.fold_in(key, 11)
    values = jax.random.truncated_normal(key, -6.0, 6.0, (SEQS, L, LATENT + ROPE), jnp.float32)
    return values.astype(jnp.bfloat16)


def draw_queries(key, part):
    key = jax.random.fold_in(key, 23)
    values = 1.5 * jax.random.truncated_normal(key, -4.0, 4.0, (STEPS, SEQS, HEADS, LATENT + ROPE), jnp.float32)
    return values.astype(jnp.bfloat16)


def shard_levels(rng, dims, cuts, smallest, top_value):
    level = 1.0
    for dim, parts in cuts:
        heights = jax.random.uniform(jax.random.fold_in(jax.random.fold_in(rng, 6), dim), (parts,), jnp.float32, smallest / len(cuts), top_value / len(cuts))
        level = level * jnp.repeat(jnp.exp(heights), dims[dim] // parts).reshape((-1,) + (1,) * (len(dims) - 1 - dim))
    return level


def length_profile(amount, total, reach, lean):
    portions = [(1 << 20) // math.isqrt(standing ** lean) + 1 for standing in range(2, amount + 1)]
    surplus, given = total - reach - (amount - 1), [1] * (amount - 1)
    while surplus > 0:
        candidates = [i for i in range(amount - 1) if given[i] < reach]
        pool, remaining = sum([portions[i] for i in candidates]), surplus
        for i in candidates:
            extra = min(reach - given[i], max(1, remaining * portions[i] // pool), surplus)
            given[i] = given[i] + extra
            surplus = surplus - extra
    return np.array([reach] + given)


def uneven_parts(stream_key, amount, total, most, skew):
    if amount == 2:
        one = jax.random.randint(stream_key, (), max(1, total - most), min(most, total - 1) + 1)
        return jnp.stack([one, total - one])
    sizes = jnp.asarray(length_profile(amount, total, most, skew), jnp.int32)
    couples = (amount - 1) // 2
    donor, sink = sizes[1:1 + 2 * couples:2], sizes[2:2 + 2 * couples:2]
    margin = jnp.minimum(donor - 1, most - sink)
    passed = jax.random.randint(jax.random.fold_in(stream_key, 1), (couples,), 0, 1 << 20) % (margin + 1)
    sizes = sizes.at[1:1 + 2 * couples:2].set(donor - passed).at[2:2 + 2 * couples:2].set(sink + passed)
    return sizes[jax.random.permutation(jax.random.fold_in(stream_key, 2), amount)]


def routed_block(key, own, number, rows, number_of, top, bound, skew):
    ranking = jax.random.permutation(key, number_of)
    crowded, usual = shares(number_of, rows * top, bound, skew, True), shares(number_of, rows * top, bound, skew, False)
    places = jnp.arange(number_of)

    def named(tallies, rotation):
        used = int((tallies > 0).sum())
        fixed = max(1, used // 4)
        passed = fixed + (places - fixed + rotation * (used - fixed)) % max(1, number_of - fixed)
        return jnp.zeros((number_of,), jnp.int32).at[ranking[jnp.where(places < fixed, places, passed)]].set(jnp.asarray(tallies, jnp.int32))

    tallies = jnp.where(number % 4 == 0, named(crowded, number // 4), named(usual, number - number // 4 - 1))
    mixed = jax.random.permutation(jax.random.fold_in(own, 3), number_of)
    donor, sink = mixed[0:number_of // 2 * 2:2], mixed[1:number_of // 2 * 2:2]
    room = jnp.minimum(tallies[donor] - 1, bound - tallies[sink]) // 2
    room = jnp.where((donor == ranking[0]) | (sink == ranking[0]) | (tallies[sink] == 0), 0, jnp.maximum(room, 0))
    passed = jax.random.randint(jax.random.fold_in(own, 4), (number_of // 2,), 0, 1 << 20) % (room + 1)
    tallies = tallies.at[donor].add(-passed).at[sink].add(passed)
    labels = jnp.searchsorted(jnp.cumsum(tallies), jnp.arange(rows * top), side="right").astype(jnp.int32)
    listing = labels.reshape(top, rows).T
    listing = listing[jax.random.permutation(jax.random.fold_in(own, 1), rows)]
    rotation = jax.random.randint(jax.random.fold_in(own, 2), (rows, 1), 0, top)
    return jnp.take_along_axis(listing, (jnp.arange(top)[None, :] + rotation) % top, axis=1)


def shares(count, total, limit, skew, full):
    weights = [(1 << 20) // math.isqrt(standing ** skew) + 1 for standing in range(1, count + 1)]
    largest = limit if full else min(limit, max(-(-total // count), total * weights[0] // sum(weights)))
    least = 1 if total - largest >= count - 1 else 0
    given, surplus = [largest] + [least] * (count - 1), total - largest - least * (count - 1)
    while surplus > 0:
        movable = [i for i in range(1, count) if given[i] < largest] or [i for i in range(1, count) if given[i] < limit]
        mass, left = sum([weights[i] for i in movable]), surplus
        for i in movable:
            extra = min(limit - given[i], max(1, left * weights[i] // mass), surplus)
            given[i] = given[i] + extra
            surplus = surplus - extra
    return np.array(given)


def scatter_about(rng, extent, scale, reach, pieces=(), kind=jnp.bfloat16):
    values = jax.random.normal(rng, extent, jnp.float32) * scale
    if len(pieces) > 0:
        values = shard_levels(rng, extent, pieces, -0.22, 0.18) * values
    return jnp.clip(values, min=-reach, max=reach).astype(kind)


def setup_inputs(seed: int = 0) -> dict:
    splits = jax.random.split(jax.random.key(seed), 9)
    queries = draw_queries(jax.random.fold_in(splits[8], 71), 0)
    latent_cache = draw_latent_cache(jax.random.fold_in(splits[8], 71), 0)
    cache_lengths = uneven_parts(splits[2], SEQS, SEQS * (L - STEPS) // 2, L - STEPS, 1).astype(jnp.int32)
    hidden_acts = scatter_about(splits[3], (TOKENS, TOP_F, FFN), 1.0, 6.0, ((0, 512),))
    routes_keys = jax.random.split(jax.random.fold_in(splits[4], 1), TOKENS // TOK_DEV)
    routes_turns = jax.random.permutation(jax.random.fold_in(splits[4], 3), TOKENS // TOK_DEV)
    routes = jax.vmap(lambda own, number: routed_block(jax.random.fold_in(splits[4], 2), own, number, TOK_DEV, EXPERTS_F, TOP_F, MOST, 1))(routes_keys, routes_turns).reshape((TOKENS, TOP_F))
    route_weights = jnp.clip(0.2 + 0.8 * jax.random.uniform(splits[5], (TOKENS, TOP_F), jnp.float32) ** shard_levels(splits[5], (TOKENS, TOP_F), ((0, 512),), -0.2, 0.2), 0.2, 1.0)
    stored_values = scatter_about(splits[6], (EXPERTS_F, FFN, D), FFN ** -0.5, 0.125, ((0, 32), (1, 32)))
    block_scales = jnp.clip(jnp.exp(math.log(4.0) - 2.7725887 * jax.random.uniform(splits[7], (EXPERTS_F, FFN // QB, D // QB), jnp.float32) ** shard_levels(splits[7], (EXPERTS_F, FFN // QB, D // QB), ((0, 32),), -0.2, 0.2)), 0.25, 4.0)
    return {"queries": queries, "latent_cache": latent_cache, "cache_lengths": cache_lengths, "hidden_acts": hidden_acts, "routes": routes, "route_weights": route_weights, "stored_values": stored_values, "block_scales": block_scales}


SCORE_SCALE = 192.0 ** -0.5


def attend_one(packed):
    query_block, key_rows, length = packed
    scores = jnp.einsum('shw,pw->shp', query_block.astype(jnp.float32), key_rows.astype(jnp.float32)) * SCORE_SCALE
    position = lax.broadcasted_iota(jnp.int32, (STEPS, 1, L), 2)
    allowed = length + lax.broadcasted_iota(jnp.int32, (STEPS, 1, 1), 0) + 1
    scores = jnp.where(position < allowed, scores, -jnp.inf)
    peak = jnp.max(scores, axis=-1, keepdims=True)
    raised = jnp.exp(scores - peak)
    denominator = jnp.sum(raised, axis=-1, keepdims=True)
    weights = (raised / denominator).astype(jnp.bfloat16)
    mixed_rows = jnp.einsum('shp,pc->shc', weights.astype(jnp.float32), key_rows[:, :LATENT].astype(jnp.float32))
    return mixed_rows.astype(jnp.bfloat16)


def dequantize(packed):
    values, scales = packed
    scale_grid = jnp.repeat(jnp.repeat(scales, QB, axis=0), QB, axis=1)
    return (values.astype(jnp.float32) * scale_grid).astype(jnp.bfloat16)


def reference(queries, latent_cache, cache_lengths, hidden_acts, routes, route_weights, stored_values, block_scales):
    attended = lax.map(attend_one, (jnp.moveaxis(queries, 1, 0), latent_cache, cache_lengths.astype(jnp.int32)))
    attended = jnp.moveaxis(attended, 0, 1)
    synced = lax.map(dequantize, (stored_values, block_scales))
    pair_count = TOKENS * TOP_F
    flat_routes = jnp.concatenate([routes.reshape(pair_count).astype(jnp.int32), jnp.full((1,), -1, jnp.int32)])
    flat_acts = jnp.concatenate([hidden_acts.reshape(pair_count, FFN), jnp.zeros((1, FFN), jnp.bfloat16)])
    flat_weights = jnp.concatenate([route_weights.reshape(pair_count), jnp.zeros((1,), jnp.float32)])
    capacity = N_REPLICA * N_EXPERT * MOST

    def expert_step(running, packed):
        expert, matrix = packed
        chosen = jnp.nonzero(flat_routes == expert, size=capacity, fill_value=pair_count)[0].astype(jnp.int32)
        selected = flat_acts[chosen]
        product = jnp.dot(selected, matrix, preferred_element_type=jnp.float32).astype(jnp.bfloat16)
        contribution = product.astype(jnp.float32) * flat_weights[chosen][:, None]
        contribution = jnp.where((chosen < pair_count)[:, None], contribution, jnp.float32(0.0))
        return running.at[chosen].add(contribution), None

    running = jnp.zeros((pair_count + 1, D), jnp.float32)
    running, unused = lax.scan(expert_step, running, (jnp.arange(EXPERTS_F, dtype=jnp.int32), synced))
    combined = jnp.sum(running[:pair_count].reshape(TOKENS, TOP_F, D), axis=1).astype(jnp.bfloat16)
    expert_output = combined.reshape(TOKENS, D // (N_TENSOR * DB), N_TENSOR, DB)
    return attended, synced, expert_output
```

```python
import functools

import jax
import jax.numpy as jnp
from jax import lax
from jax.experimental import pallas as pl
from jax.experimental.pallas import tpu as pltpu
from jax.sharding import PartitionSpec as P

XH = 2
XL = 4
SLOTS = 2
QB = 128
ROPE = 64
SCORE_SCALE = 192.0 ** (-0.5)
LANES = 128
MESH = pl.DeviceIdType.MESH
F32 = jnp.float32
BF16 = jnp.bfloat16


def iota(shape, axis):
    return lax.broadcasted_iota(jnp.int32, shape, axis)


def onehot(mask):
    return jnp.where(mask, 1.0, 0.0).astype(BF16)


def kernel(
    sizes,
    lengths,
    scales,
    routes,
    weights,
    hidden,
    queries,
    cache,
    stored,
    attended,
    synced,
    gathered,
    pack_out,
    pack_in,
    wfull,
    stacked,
    y_out,
    y_in,
    x_out,
    rows,
    products,
    r_out,
    r_in,
    meta,
    f_out,
    f_in,
    perm,
    att,
    local_sem,
    send_sem,
    w_sem,
    y_sem,
    x_sem,
    right_sem,
    left_sem,
    pair_sem,
    meta_sem,
    r_sem,
    f_sem,
):
    nr, ne, nt = sizes
    nz, ny = nr // XH, ne // XL
    nx = XH * XL
    tok = routes.shape[0]
    width = stored.shape[1] // (nr * nt)
    depth = stored.shape[0]
    chunks = hidden.shape[1] // (2 * nt * LANES)
    half = chunks * LANES
    groups = max(1, nz // 4)
    per = nz // groups
    order = [0]
    for step in range(1, nz // 2):
        order += [-step, step]
    order.append(nz // 2)

    r, e, t = lax.axis_index("replica"), lax.axis_index("expert"), lax.axis_index("tensor")
    xh, z = r // nz, r % nz
    y, xl = e // XL, e % XL
    x = xh * XL + xl
    me = r * nt + t

    def to(rep, exp, ten):
        return {"replica": rep, "expert": exp, "tensor": ten}

    barrier = pltpu.get_barrier_semaphore()

    def greet(rep, exp, ten):
        pl.semaphore_signal(barrier, inc=1, device_id=to(rep, exp, ten), device_id_type=MESH)

    @pl.loop(1, nr * nt)
    def _(d):
        other = (me + d) % (nr * nt)
        greet(other // nt, e, other % nt)

    @pl.loop(1, ne)
    def _(d):
        greet(r, (e + d) % ne, t)

    for dh in range(1, XH):
        for dl in range(1, XL):
            greet((xh + dh) % XH * nz + z, y * XL + (xl + dl) % XL, t)

    named = routes[...].astype(F32)
    column = [named[:, k : k + 1] for k in range(2)]
    eye = iota((tok, tok), 0) == iota((tok, tok), 1)
    before = iota((tok, tok), 1) < iota((tok, tok), 0)
    line = [jnp.sum(jnp.where(eye, c, 0.0), axis=0, keepdims=True) for c in column]
    slot = []
    for k in range(2):
        count = jnp.sum(jnp.where((column[k] == line[k]) & before, 1.0, 0.0), axis=1, keepdims=True)
        for other in range(k):
            count += jnp.sum(jnp.where(column[k] == line[other], 1.0, 0.0), axis=1, keepdims=True)
        slot.append(count)
    pairs = 2 * tok
    block = chunks * SLOTS
    target = jnp.concatenate([column[k] * block + slot[k] for k in range(2)], axis=0)
    lane = iota((pairs, chunks * pairs), 1)
    spread = jnp.where(lane % pairs == iota((pairs, chunks * pairs), 0), target, 0.0)
    wanted = jnp.sum(spread, axis=0, keepdims=True)
    wanted = wanted + (iota((1, chunks * pairs), 1) // pairs * SLOTS).astype(F32)
    placer = onehot(iota((ne * block, chunks * pairs), 0).astype(F32) == wanted)
    for c in range(chunks):
        for k in range(2):
            start = pl.multiple_of(k * nt * half + t * half + c * LANES, LANES)
            stacked[c * pairs + k * tok : c * pairs + (k + 1) * tok, :] = hidden[:, pl.ds(start, LANES)]
    y_out[...] = (
        jnp.dot(placer, stacked[...], preferred_element_type=F32).astype(BF16).reshape(y_out.shape)
    )
    lane = iota((tok, LANES), 1)
    note = jnp.zeros((tok, LANES), F32)
    for k in range(2):
        place = column[k] * (nz * XH * SLOTS) + slot[k]
        note = jnp.where(lane == k, place, note)
        note = jnp.where(lane == 2 + k, weights[:, k : k + 1], note)
    meta[r] = note

    pl.semaphore_wait(barrier, nr * nt - 1 + ne - 1 + (XH - 1) * (XL - 1))

    @pl.loop(1, ny)
    def _(d):
        other = (y + d) % ny
        pltpu.make_async_remote_copy(
            y_out.at[other], y_in.at[y], send_sem.at[0], y_sem,
            device_id=to(r, other * XL + xl, t), device_id_type=MESH,
        ).start()

    own = pltpu.make_async_copy(y_out.at[y], y_in.at[y], local_sem.at[0])
    own.start()

    @pl.loop(1, nr)
    def _(d):
        other = (r + d) % nr
        pltpu.make_async_remote_copy(
            meta.at[r], meta.at[r], send_sem.at[1], meta_sem,
            device_id=to(other, e, t), device_id_type=MESH,
        ).start()

    window = 4 * width
    tiles = window // QB
    part = depth // 4

    @pl.loop(0, nr * nt // 4)
    def _(q):
        values = stored[:, pl.ds(pl.multiple_of(q * window, QB), window)].astype(F32)
        row = me * depth // QB
        values = jnp.concatenate(
            [values[:, j * QB : (j + 1) * QB] * scales[row, q * tiles + j] for j in range(tiles)], axis=1
        ).astype(BF16)
        for b in range(4):
            pack_out[q * 4 + b] = jnp.concatenate(
                [values[part * g : part * (g + 1), width * b : width * (b + 1)] for g in range(4)], axis=1
            )

    @pl.loop(1, nr * nt)
    def _(d):
        other = (me + d) % (nr * nt)
        pltpu.make_async_remote_copy(
            pack_out.at[other], pack_in.at[me], send_sem.at[2], w_sem,
            device_id=to(other // nt, e, other % nt), device_id_type=MESH,
        ).start()

    mine = pltpu.make_async_copy(pack_out.at[me], pack_in.at[me], local_sem.at[1])
    mine.start()

    own.wait()
    pltpu.make_async_copy(y_out.at[pl.ds(0, ny - 1)], y_in.at[pl.ds(0, ny - 1)], y_sem).wait()
    size = ny * block
    out_row, in_row = iota((size, size), 0), iota((size, size), 1)
    source = (out_row // SLOTS) % ny * block + out_row // (ny * SLOTS) * SLOTS + out_row % SLOTS
    turned = jnp.concatenate(
        [
            jnp.concatenate([y_in[k, l * block : (l + 1) * block, :] for k in range(ny)], axis=0)
            for l in range(XL)
        ],
        axis=1,
    )
    turned = jnp.dot(onehot(source == in_row), turned, preferred_element_type=F32).astype(BF16)
    for l in range(XL):
        x_out[l] = turned[:, l * LANES : (l + 1) * LANES]

    @pl.loop(1, nx)
    def _(d):
        other = (x + d) % nx
        pltpu.make_async_remote_copy(
            x_out.at[other % XL], rows.at[z, t, x], send_sem.at[3], x_sem,
            device_id=to(other // XL * nz + z, y * XL + other % XL, t), device_id_type=MESH,
        ).start()

    kept = pltpu.make_async_copy(x_out.at[xl], rows.at[z, t, x], local_sem.at[2])
    kept.start()

    steps, heads, full = queries.shape
    positions = cache.shape[0]
    scores = lax.dot_general(
        queries[...].reshape(steps * heads, full), cache[...], (((1,), (1,)), ((), ())),
        preferred_element_type=F32,
    )
    position = iota((heads, positions), 1)
    for s in range(steps):
        seen = jnp.where(
            position < lengths[0] + s + 1, scores[s * heads : (s + 1) * heads] * SCORE_SCALE, -jnp.inf
        )
        raised = jnp.exp(seen - jnp.max(seen, axis=-1, keepdims=True))
        shares = (raised / jnp.sum(raised, axis=-1, keepdims=True)).astype(BF16)
        att[s] = jnp.dot(shares, cache[:, : full - ROPE], preferred_element_type=F32).astype(BF16)
    attended_copy = pltpu.make_async_copy(att, attended, local_sem.at[3])
    attended_copy.start()

    size = per * nx * ny * SLOTS
    out_row, in_row = iota((size, 1), 0), iota((size, size), 1)
    piece = per * XH * SLOTS
    home, rest = out_row // piece, out_row % piece
    source = (
        rest // (XH * SLOTS) * (nx * ny * SLOTS)
        + (rest // SLOTS % XH * XL + home % XL) * (ny * SLOTS)
        + home // XL * SLOTS
        + rest % SLOTS
    )
    perm[...] = onehot(source == in_row)

    kept.wait()
    pltpu.make_async_copy(rows.at[0, 0, pl.ds(0, nx - 1)], rows.at[0, 0, pl.ds(0, nx - 1)], x_sem).wait()
    hx = nx // 2

    def piece_of(offset, h):
        return rows.at[(z + offset + nz) % nz, t, pl.ds(h * hx, hx)]

    def ring(offset, h, sem, direction):
        copy = pltpu.make_async_remote_copy(
            piece_of(offset, h), piece_of(offset, h), send_sem.at[4], sem,
            device_id=to(xh * nz + (z + direction + nz) % nz, e, t), device_id_type=MESH,
        )
        return copy

    def pair(index, h):
        return pltpu.make_async_remote_copy(
            piece_of(order[index], h), piece_of(order[index], h), send_sem.at[5], pair_sem.at[index, h],
            device_id=to(r, e, 1 - t), device_id_type=MESH,
        )

    def product(index):
        chunk = rows.at[(z + order[index] + nz) % nz]
        left = jnp.concatenate(
            [
                chunk[u, :, c * ny * SLOTS : (c + 1) * ny * SLOTS, :].reshape(nx * ny * SLOTS, LANES)
                for u in range(nt)
                for c in range(chunks)
            ],
            axis=1,
        )
        value = jnp.dot(left, wfull[...], preferred_element_type=F32).astype(BF16)
        where = index % per * (nx * ny * SLOTS)
        products[where : where + nx * ny * SLOTS, :width] = value

    def unpack():
        mine.wait()
        pltpu.make_async_copy(
            pack_out.at[pl.ds(0, nr * nt - 1)], pack_in.at[pl.ds(0, nr * nt - 1)], w_sem
        ).wait()

        @pl.loop(0, nr * nt)
        def _(s):
            values = pack_in[s]
            for g in range(4):
                start = pl.multiple_of(s * depth + g * part, part)
                wfull[pl.ds(start, part), :] = values[:, width * g : width * (g + 1)]

    def send_back(group):
        value = jnp.dot(perm[...], products[...], preferred_element_type=F32).astype(BF16)
        r_out[group] = value.reshape(r_out.shape[1:])

        @pl.loop(1, ne)
        def _(d):
            other = (e + d) % ne
            pltpu.make_async_remote_copy(
                r_out.at[group, other], r_in.at[group, e], send_sem.at[6], r_sem.at[group],
                device_id=to(r, other, t), device_id_type=MESH,
            ).start()

        here = pltpu.make_async_copy(r_out.at[group, e], r_in.at[group, e], local_sem.at[5])
        here.start()
        here.wait()

    products[...] = jnp.zeros_like(products)
    last = nz // 2
    synced_copy = pltpu.make_async_copy(wfull, synced, local_sem.at[4])
    for step in range(last + 1):
        if step == 0:
            for h in range(2):
                ring(0, h, right_sem.at[0, h], 1).start()
                ring(0, h, left_sem.at[0, h], -1).start()
            for h in range(2):
                pair(0, h).start()
        else:
            for h in range(2):
                if step < last or h == 0:
                    ring(-step, h, right_sem.at[step - 1, h], 1).wait_recv()
                    if step + 1 < last or (step + 1 == last and h == 0):
                        ring(-step, h, right_sem.at[step, h], 1).start()
                    pair(2 * step - 1, h).start()
                if step < last or h == 1:
                    ring(step, h, left_sem.at[step - 1, h], -1).wait_recv()
                    if step + 1 < last or (step + 1 == last and h == 1):
                        ring(step, h, left_sem.at[step, h], -1).start()
                    pair(2 * step if step < last else 2 * step - 1, h).start()
        if step == 0:
            unpack()
            synced_copy.start()
        ready = [0] if step == 0 else [2 * step - 1, 2 * step] if step < last else [2 * step - 1]
        for index in ready:
            for h in range(2):
                pair(index, h).wait_recv()
            product(index)
            if index % per == per - 1:
                send_back(index // per)

    pltpu.make_async_copy(meta.at[pl.ds(0, nr - 1)], meta.at[pl.ds(0, nr - 1)], meta_sem).wait()
    for group in range(groups):
        pltpu.make_async_copy(
            r_out.at[group, pl.ds(0, ne - 1)], r_in.at[group, pl.ds(0, ne - 1)], r_sem.at[group]
        ).wait()
    arrived = [r_in[group].reshape(ne * piece, r_in.shape[-1]) for group in range(groups)]
    position = iota((tok, ne * piece), 1).astype(F32)
    for index in range(nz):
        group = index // per
        for h in range(XH):
            home = h * nz + (z + order[index] + nz) % nz
            facts = meta[home]
            total = jnp.zeros((tok, r_in.shape[-1]), F32)
            picks = []
            for k in range(2):
                place = facts[:, k : k + 1]
                place = jnp.floor(place * (1.0 / (nz * XH * SLOTS))) * piece + (
                    place - jnp.floor(place * (1.0 / (nz * XH * SLOTS))) * (nz * XH * SLOTS)
                )
                place = place + (index % per * XH * SLOTS + h * SLOTS)
                picks.append(onehot(position == place))
            picked = jnp.dot(jnp.concatenate(picks, axis=0), arrived[group], preferred_element_type=F32)
            for k in range(2):
                total += picked[k * tok : (k + 1) * tok] * facts[:, 2 + k : 3 + k]
            f_out[home] = total.astype(BF16)

    @pl.loop(1, nr)
    def _(d):
        other = (r + d) % nr
        pltpu.make_async_remote_copy(
            f_out.at[other], f_in.at[r], send_sem.at[7], f_sem,
            device_id=to(other, e, t), device_id_type=MESH,
        ).start()

    final = pltpu.make_async_copy(f_out.at[r], f_in.at[r], local_sem.at[0])
    final.start()
    final.wait()

    def sent(ref, number):
        pltpu.make_async_copy(ref, ref, send_sem.at[number]).wait()

    sent(y_out.at[pl.ds(0, ny - 1)], 0)
    sent(meta.at[pl.ds(0, nr - 1)], 1)
    sent(pack_out.at[pl.ds(0, nr * nt - 1)], 2)
    sent(rows.at[0, 0, pl.ds(0, nx - 1)], 3)
    sent(rows.at[pl.ds(0, nz - 1), 0], 4)
    sent(rows.at[:, 0], 5)
    for group in range(groups):
        sent(r_out.at[group, pl.ds(0, ne - 1)], 6)
    sent(f_out.at[pl.ds(0, nr - 1)], 7)
    attended_copy.wait()
    synced_copy.wait()
    pltpu.make_async_copy(f_out.at[pl.ds(0, nr - 1)], f_in.at[pl.ds(0, nr - 1)], f_sem).wait()
    done = pltpu.make_async_copy(f_in, gathered, local_sem.at[1])
    done.start()
    done.wait()


def local(sizes, queries, latent_cache, cache_lengths, hidden_acts, routes, route_weights, stored_values, block_scales):
    nr, ne, nt = sizes
    nz, ny, nx = nr // XH, ne // XL, XH * XL
    steps, _, heads, full = queries.shape
    tok, _, ffn = hidden_acts.shape
    depth, columns = stored_values.shape[1:]
    width = columns // (nr * nt)
    padded = -(-width // LANES) * LANES
    chunks = ffn // (nt * LANES)
    block = chunks * SLOTS
    groups = max(1, nz // 4)
    per = nz // groups
    piece = per * XH * SLOTS
    size = nx * ny * SLOTS
    vmem = pl.BlockSpec(memory_space=pltpu.VMEM)
    smem = pl.BlockSpec(memory_space=pltpu.SMEM)
    hbm = pl.BlockSpec(memory_space=pl.ANY)
    dma = pltpu.SemaphoreType.DMA
    attended, synced, gathered = pl.pallas_call(
        functools.partial(kernel, sizes),
        out_shape=[
            jax.ShapeDtypeStruct((steps, heads, full - ROPE), BF16),
            jax.ShapeDtypeStruct((ffn, width), BF16),
            jax.ShapeDtypeStruct((nr, tok, padded), BF16),
        ],
        in_specs=[smem, smem, vmem, vmem, vmem, vmem, vmem, vmem],
        out_specs=[hbm, hbm, hbm],
        scratch_shapes=[
            pltpu.VMEM((nr * nt, depth // 4, 4 * width), BF16),
            pltpu.VMEM((nr * nt, depth // 4, 4 * width), BF16),
            pltpu.VMEM((ffn, width), BF16),
            pltpu.VMEM((chunks * 2 * tok, LANES), BF16),
            pltpu.VMEM((ny, XL * block, LANES), BF16),
            pltpu.VMEM((ny, XL * block, LANES), BF16),
            pltpu.VMEM((XL, ny * block, LANES), BF16),
            pltpu.VMEM((nz, nt, nx, ny * block, LANES), BF16),
            pltpu.VMEM((per * size, padded), BF16),
            pltpu.VMEM((groups, ne, piece, padded), BF16),
            pltpu.VMEM((groups, ne, piece, padded), BF16),
            pltpu.VMEM((nr, tok, LANES), F32),
            pltpu.VMEM((nr, tok, padded), BF16),
            pltpu.VMEM((nr, tok, padded), BF16),
            pltpu.VMEM((per * size, per * size), BF16),
            pltpu.VMEM((steps, heads, full - ROPE), BF16),
            dma((6,)),
            dma((8,)),
            dma,
            dma,
            dma,
            dma((nz // 2, 2)),
            dma((nz // 2, 2)),
            dma((nz, 2)),
            dma,
            dma((groups,)),
            dma,
        ],
        compiler_params=pltpu.CompilerParams(
            collective_id=0, has_side_effects=True, vmem_limit_bytes=56 * 1024 * 1024
        ),
        cost_estimate=pl.CostEstimate(flops=2_000_000_000, bytes_accessed=6_000_000, transcendentals=262144),
    )(
        cache_lengths,
        block_scales[0],
        routes,
        route_weights,
        hidden_acts.reshape(tok, 2 * ffn),
        queries.reshape(steps, heads, full),
        latent_cache[0],
        stored_values[0],
    )
    expert_output = jnp.transpose(gathered[:, :, :width], (1, 0, 2)).reshape(tok, nr, 1, width)
    return attended.reshape(steps, 1, heads, full - ROPE), synced[None], expert_output


def solution(mesh):
    sizes = (mesh.shape["replica"], mesh.shape["expert"], mesh.shape["tensor"])
    placed = (
        P(None, ("replica", "expert"), "tensor", None),
        P(("replica", "expert"), None, None),
        P(("replica", "expert")),
        P(("replica", "expert"), None, None),
        P(("replica", "expert"), None),
        P(("replica", "expert"), None),
        P("expert", ("replica", "tensor"), None),
        P("expert", None, None),
    )
    return jax.shard_map(
        functools.partial(local, sizes),
        mesh=mesh,
        in_specs=placed,
        out_specs=(
            P(None, ("replica", "expert"), "tensor", None),
            P("expert", None, ("replica", "tensor")),
            P(("replica", "expert"), None, "tensor", None),
        ),
        check_vma=False,
    )
```

```python
import functools

import jax
import jax.numpy as jnp
from jax import lax
from jax.experimental import pallas as pl
from jax.experimental.pallas import tpu as pltpu
from jax.sharding import PartitionSpec as P

XH = 2
XL = 4
SLOTS = 2
QB = 128
ROPE = 64
SCORE_SCALE = 192.0 ** (-0.5)
LANES = 128
PER = 2
MESH = pl.DeviceIdType.MESH
F32 = jnp.float32
BF16 = jnp.bfloat16


def iota(shape, axis):
    return lax.broadcasted_iota(jnp.int32, shape, axis)


def log2(n):
    return n.bit_length() - 1


def onehot(mask):
    return jnp.where(mask, 1.0, 0.0).astype(BF16)


def settle(ref, sem):
    pltpu.make_async_copy(ref, ref, sem).wait()


def kernel(
    sizes,
    lengths,
    scales,
    routes,
    weights,
    hidden,
    queries,
    cache,
    stored,
    attended,
    synced,
    gathered,
    pack_out,
    pack_in,
    wfull,
    stacked,
    y_out,
    y_in,
    x_out,
    rows,
    products,
    r_out,
    r_in,
    meta,
    pick,
    gains,
    f_out,
    f_in,
    final,
    perm,
    scores,
    att,
    local_sem,
    send_sem,
    w_sem,
    y_sem,
    x_sem,
    right_sem,
    left_sem,
    pair_sem,
    meta_sem,
    r_sem,
    f_sem,
):
    nr, ne, nt = sizes
    nz, ny = nr // XH, ne // XL
    nx = XH * XL
    tok = routes.shape[1]
    depth = stored.shape[0]
    width = stored.shape[1] // (nr * nt)
    chunks = hidden.shape[2] // (nt * LANES)
    half = chunks * LANES
    groups = nz // PER
    per = PER
    block = chunks * SLOTS
    line_rows = ny * SLOTS
    chunk_rows = nx * line_rows
    piece = per * XH * SLOTS
    halves = products.shape[1] // LANES
    order = [0]
    for step in range(1, nz // 2):
        order += [-step, step]
    order.append(nz // 2)

    r, e, t = lax.axis_index("replica"), lax.axis_index("expert"), lax.axis_index("tensor")
    xh, z = r // nz, r % nz
    y, xl = e // XL, e % XL
    x = xh * XL + xl
    me = r * nt + t

    def to(rep, exp, ten):
        return {"replica": rep, "expert": exp, "tensor": ten}

    def remote(src, dst, send, recv, target):
        return pltpu.make_async_remote_copy(
            src, dst, send_sem.at[send], recv, device_id=target, device_id_type=MESH
        )

    barrier = pltpu.get_barrier_semaphore()

    def greet(rep, exp, ten):
        pl.semaphore_signal(barrier, inc=1, device_id=to(rep, exp, ten), device_id_type=MESH)

    @pl.loop(1, nr * nt)
    def _(d):
        other = (me + d) % (nr * nt)
        greet(other // nt, e, other % nt)

    @pl.loop(1, ne)
    def _(d):
        greet(r, (e + d) % ne, t)

    for dh in range(1, XH):
        for dl in range(1, XL):
            greet((xh + dh) % XH * nz + z, y * XL + (xl + dl) % XL, t)

    named = routes[...].astype(F32)
    line = [named[k : k + 1, :] for k in range(2)]
    eye = iota((tok, tok), 0) == iota((tok, tok), 1)
    before = iota((tok, tok), 1) < iota((tok, tok), 0)
    column = [jnp.sum(jnp.where(eye, v, 0.0), axis=1, keepdims=True) for v in line]
    gain = [jnp.sum(jnp.where(eye, weights[k : k + 1, :], 0.0), axis=1, keepdims=True) for k in range(2)]
    slot = []
    for k in range(2):
        count = jnp.sum(jnp.where((column[k] == line[k]) & before, 1.0, 0.0), axis=1, keepdims=True)
        for other in range(k):
            count += jnp.sum(jnp.where(column[k] == line[other], 1.0, 0.0), axis=1, keepdims=True)
        slot.append(count)
    pairs = 2 * tok
    target = jnp.concatenate([column[k] * block + slot[k] for k in range(2)], axis=0)
    lane = iota((pairs, chunks * pairs), 1)
    spread = jnp.where((lane & (pairs - 1)) == iota((pairs, chunks * pairs), 0), target, 0.0)
    wanted = jnp.sum(spread, axis=0, keepdims=True)
    wanted = wanted + ((iota((1, chunks * pairs), 1) >> log2(pairs)) * SLOTS).astype(F32)
    placer = onehot(iota((ne * block, chunks * pairs), 0).astype(F32) == wanted)
    for c in range(chunks):
        start = pl.multiple_of(t * half + c * LANES, LANES)
        part = hidden[:, :, pl.ds(start, LANES)]
        for k in range(2):
            stacked[c * pairs + k * tok : c * pairs + (k + 1) * tok, :] = part[:, k, :]
    y_out[...] = (
        jnp.dot(placer, stacked[...], preferred_element_type=F32).astype(BF16).reshape(y_out.shape)
    )
    lane = iota((tok, LANES), 1)
    note = jnp.zeros((tok, LANES), F32)
    for k in range(2):
        note = jnp.where(lane == k, column[k] * piece + slot[k], note)
        note = jnp.where(lane == 2 + k, gain[k], note)
    meta[r] = note

    window = 4 * width
    tiles = window // QB
    high = width // 2

    @pl.loop(0, nr * nt // 4)
    def _(q):
        values = stored[:, pl.ds(pl.multiple_of(q * window, QB), window)].astype(F32)
        row = me * depth // QB
        values = jnp.concatenate(
            [values[:, j * QB : (j + 1) * QB] * scales[row, q * tiles + j] for j in range(tiles)], axis=1
        ).astype(BF16)
        values = values.T
        for b in range(4):
            pack_out[q * 4 + b] = jnp.concatenate(
                [values[width * b + high * g : width * b + high * (g + 1), :] for g in range(2)], axis=1
            )

    pl.semaphore_wait(barrier, nr * nt - 1 + ne - 1 + (XH - 1) * (XL - 1))

    @pl.loop(1, ny)
    def _(d):
        other = (y + d) % ny
        remote(y_out.at[other], y_in.at[y], 0, y_sem, to(r, other * XL + xl, t)).start()

    own = pltpu.make_async_copy(y_out.at[y], y_in.at[y], local_sem.at[0])
    own.start()

    def send_weights(first, end):
        @pl.loop(first, end)
        def _(d):
            other = (me + d) % (nz * nt) + (xh + d // (nz * nt)) % XH * (nz * nt)
            remote(pack_out.at[other], pack_in.at[me], 2, w_sem, to(other // nt, e, other % nt)).start()

    send_weights(1, nz * nt)
    mine = pltpu.make_async_copy(pack_out.at[me], pack_in.at[me], local_sem.at[1])
    mine.start()

    size = ny * block
    out_row, in_row = iota((size, 1), 0), iota((size, size), 1)
    source = (
        ((out_row >> log2(SLOTS)) & (ny - 1)) * block
        + (out_row >> log2(line_rows)) * SLOTS
        + (out_row & (SLOTS - 1))
    )
    turn = onehot(source == in_row)
    own.wait()
    settle(y_in.at[pl.ds(0, ny - 1)], y_sem)
    turned = jnp.concatenate(
        [
            jnp.concatenate([y_in[k, l * block : (l + 1) * block, :] for k in range(ny)], axis=0)
            for l in range(XL)
        ],
        axis=1,
    )
    turned = jnp.dot(turn, turned, preferred_element_type=F32).astype(BF16)
    for l in range(XL):
        x_out[l] = turned[:, l * LANES : (l + 1) * LANES]

    @pl.loop(1, nx)
    def _(d):
        other = (x + d) % nx
        target = to(other // XL * nz + z, y * XL + other % XL, t)
        remote(x_out.at[other % XL], rows.at[z, t, x], 3, x_sem, target).start()

    kept = pltpu.make_async_copy(x_out.at[xl], rows.at[z, t, x], local_sem.at[2])
    kept.start()
    send_weights(nz * nt, nr * nt)

    @pl.loop(1, nr)
    def _(d):
        other = (r + d) % nr
        remote(meta.at[r], meta.at[r], 1, meta_sem, to(other, e, t)).start()

    steps, heads, full = queries.shape
    positions = cache.shape[1]

    def score():
        scores[...] = jnp.dot(
            queries[...].reshape(steps * heads, full), cache[...], preferred_element_type=F32
        )

    def attend(s):
        position = iota((1, positions), 1)
        seen = jnp.where(
            position < lengths[0] + s + 1, scores[s * heads : (s + 1) * heads] * SCORE_SCALE, -jnp.inf
        )
        raised = jnp.exp(seen - jnp.max(seen, axis=-1, keepdims=True))
        shares = raised * (1.0 / jnp.sum(raised, axis=-1, keepdims=True))
        att[s] = lax.dot_general(
            shares.astype(BF16), cache[: full - ROPE, :], (((1,), (1,)), ((), ())),
            preferred_element_type=F32,
        ).astype(BF16)

    def permute():
        size = per * chunk_rows
        out_row, in_row = iota((size, 1), 0), iota((size, size), 1)
        home, rest = out_row >> log2(piece), out_row & (piece - 1)
        source = (
            (rest >> log2(XH * SLOTS)) * chunk_rows
            + (((rest >> log2(SLOTS)) & (XH - 1)) * XL + (home & (XL - 1))) * line_rows
            + (home >> log2(XL)) * SLOTS
            + (rest & (SLOTS - 1))
        )
        perm[...] = onehot(source == in_row)

    def homes(group):
        for index in range(group * per, (group + 1) * per):
            for h in range(XH):
                yield index - group * per, h, h * nz + (z + order[index] + nz) % nz

    def prepare(group):
        position = iota((tok, ne * piece), 1).astype(F32)
        for index, h, home in homes(group):
            facts = meta[home]
            for k in range(2):
                start = ((index * XH + h) * 2 + k) * tok
                place = facts[:, k : k + 1] + (index * XH + h) * SLOTS
                pick[group, start : start + tok, :] = onehot(position == place)
                gains[group, start : start + tok, :] = facts[:, 2 + k : 3 + k]

    hx = nx // 2

    def piece_of(offset, h):
        return rows.at[(z + offset + nz) % nz, t, pl.ds(h * hx, hx)]

    def ring(offset, h, sem, direction):
        target = to(xh * nz + (z + direction + nz) % nz, e, t)
        return remote(piece_of(offset, h), piece_of(offset, h), 4, sem, target)

    def pair(index, h):
        ref = piece_of(order[index], h)
        return remote(ref, ref, 5, pair_sem.at[index, h], to(r, e, 1 - t))

    def product(first, end):
        for index in range(first, end):
            for h in range(2):
                pair(index, h).wait_recv()
        lefts = []
        for index in range(first, end):
            chunk = rows.at[(z + order[index] + nz) % nz]
            lefts.append(
                jnp.concatenate(
                    [
                        chunk[u, :, c * line_rows : (c + 1) * line_rows, :].reshape(chunk_rows, LANES)
                        for u in range(nt)
                        for c in range(chunks)
                    ],
                    axis=1,
                )
            )
        value = lax.dot_general(
            jnp.concatenate(lefts, axis=0), wfull[...], (((1,), (1,)), ((), ())),
            preferred_element_type=F32,
        ).astype(BF16)
        where = first % per * chunk_rows
        products[where : where + (end - first) * chunk_rows, :width] = value

    def unpack():
        mine.wait()
        settle(pack_in.at[pl.ds(0, nr * nt - 1)], w_sem)

        @pl.loop(0, nr)
        def _(s):
            values = [pack_in[s * nt + u] for u in range(nt)]
            for g in range(2):
                wfull[high * g : high * (g + 1), pl.ds(pl.multiple_of(s * nt * depth, nt * depth), nt * depth)] = (
                    jnp.concatenate([v[:, depth * g : depth * (g + 1)] for v in values], axis=1)
                )

    def send_back(group):
        value = jnp.dot(perm[...], products[...], preferred_element_type=F32).astype(BF16)
        for g in range(halves):
            r_out[group, :, g * piece : (g + 1) * piece, :] = value[:, g * LANES : (g + 1) * LANES].reshape(
                ne, piece, LANES
            )

        @pl.loop(1, ne)
        def _(d):
            other = (e + d) % ne
            remote(r_out.at[group, other], r_in.at[group, e], 6, r_sem.at[group], to(r, other, t)).start()

        here = pltpu.make_async_copy(r_out.at[group, e], r_in.at[group, e], local_sem.at[5])
        here.start()
        here.wait()

    def combine(group):
        settle(r_in.at[group, pl.ds(0, ne - 1)], r_sem.at[group])
        arrived = r_in[group]
        arrived = jnp.concatenate(
            [arrived[:, g * piece : (g + 1) * piece, :].reshape(ne * piece, LANES) for g in range(halves)], axis=1
        )
        picked = jnp.dot(pick[group], arrived, preferred_element_type=F32) * gains[group]
        for index, h, home in homes(group):
            start = (index * XH + h) * 2 * tok
            f_out[home] = (picked[start : start + tok] + picked[start + tok : start + 2 * tok]).astype(BF16)
        for index, h, home in homes(group):
            if group == 0 and index == 0:
                @pl.when(h == xh)
                def _():
                    f_in[home] = f_out[home]

                @pl.when(h != xh)
                def _():
                    remote(f_out.at[home], f_in.at[r], 7, f_sem, to(home, e, t)).start()
            else:
                remote(f_out.at[home], f_in.at[r], 7, f_sem, to(home, e, t)).start()

    last = nz // 2

    def when(index):
        return min(last, max(2, (index + 1) // 2))

    def forward(step):
        for h in range(2):
            if step == 0:
                ring(0, h, right_sem.at[0, h], 1).start()
                ring(0, h, left_sem.at[0, h], -1).start()
                pair(0, h).start()
                continue
            if step < last or h == 0:
                ring(-step, h, right_sem.at[step - 1, h], 1).wait_recv()
                if step + 1 < last or (step + 1 == last and h == 0):
                    ring(-step, h, right_sem.at[step, h], 1).start()
                pair(2 * step - 1, h).start()
            if step < last or h == 1:
                ring(step, h, left_sem.at[step - 1, h], -1).wait_recv()
                if step + 1 < last or (step + 1 == last and h == 1):
                    ring(step, h, left_sem.at[step, h], -1).start()
                pair(2 * step if step < last else 2 * step - 1, h).start()

    score()
    kept.wait()
    settle(rows.at[0, 0, pl.ds(0, nx - 1)], x_sem)
    forward(0)
    for s in range(steps):
        attend(s)
    attended_copy = pltpu.make_async_copy(att, attended, local_sem.at[3])
    attended_copy.start()
    permute()
    settle(meta.at[pl.ds(0, nr - 1)], meta_sem)
    for group in range(groups):
        prepare(group)
    products[...] = jnp.zeros_like(products)
    for step in range(1, last + 1):
        forward(step)
        if step == min(2, last):
            unpack()
            synced_copy = pltpu.make_async_copy(wfull, synced, local_sem.at[4])
            synced_copy.start()
        for group in range(groups):
            first, end = group * per, (group + 1) * per
            if step == when(end - 1):
                if first < end - 1 and step > when(end - 2):
                    product(end - 1, end)
                else:
                    product(first, end)
                send_back(group)
            elif step == when(end - 2):
                product(first, end - 1)
        if step == last - 1:
            for group in range(groups - 3):
                combine(group)
    for group in range(max(0, groups - 3), groups):
        combine(group)

    settle(y_out.at[pl.ds(0, ny - 1)], send_sem.at[0])
    settle(meta.at[pl.ds(0, nr - 1)], send_sem.at[1])
    settle(pack_out.at[pl.ds(0, nr * nt - 1)], send_sem.at[2])
    settle(rows.at[0, 0, pl.ds(0, nx - 1)], send_sem.at[3])
    settle(rows.at[pl.ds(0, nz - 1), 0], send_sem.at[4])
    settle(rows.at[:, 0], send_sem.at[5])
    for group in range(groups):
        settle(r_out.at[group, pl.ds(0, ne - 1)], send_sem.at[6])
    settle(f_out.at[pl.ds(0, nr - 1)], send_sem.at[7])
    attended_copy.wait()
    synced_copy.wait()
    settle(f_in.at[pl.ds(0, nr - 1)], f_sem)
    size = nr * tok
    out_row, in_row = iota((size, 1), 0), iota((size, size), 1)
    source = (out_row & (nr - 1)) * tok + (out_row >> log2(nr))
    value = jnp.dot(
        onehot(source == in_row), f_in[...].reshape(size, f_in.shape[2]), preferred_element_type=F32
    )
    final[...] = value[:, :width].astype(BF16).reshape(tok, nr, width)
    result = pltpu.make_async_copy(final, gathered, local_sem.at[1])
    result.start()
    result.wait()


def local(sizes, queries, latent_cache, cache_lengths, hidden_acts, routes, route_weights, stored_values, block_scales):
    nr, ne, nt = sizes
    nz, ny, nx = nr // XH, ne // XL, XH * XL
    steps, _, heads, full = queries.shape
    tok, _, ffn = hidden_acts.shape
    depth, columns = stored_values.shape[1:]
    width = columns // (nr * nt)
    padded = -(-width // LANES) * LANES
    chunks = ffn // (nt * LANES)
    block = chunks * SLOTS
    groups = nz // PER
    per = PER
    piece = per * XH * SLOTS
    size = nx * ny * SLOTS
    vmem = pl.BlockSpec(memory_space=pltpu.VMEM)
    smem = pl.BlockSpec(memory_space=pltpu.SMEM)
    hbm = pl.BlockSpec(memory_space=pl.ANY)
    dma = pltpu.SemaphoreType.DMA
    attended, synced, gathered = pl.pallas_call(
        functools.partial(kernel, sizes),
        out_shape=[
            jax.ShapeDtypeStruct((steps, heads, full - ROPE), BF16),
            jax.ShapeDtypeStruct((width, ffn), BF16),
            jax.ShapeDtypeStruct((tok, nr, width), BF16),
        ],
        in_specs=[smem, smem, vmem, vmem, vmem, vmem, vmem, vmem],
        out_specs=[hbm, hbm, hbm],
        scratch_shapes=[
            pltpu.VMEM((nr * nt, width // 2, 2 * depth), BF16),
            pltpu.VMEM((nr * nt, width // 2, 2 * depth), BF16),
            pltpu.VMEM((width, ffn), BF16),
            pltpu.VMEM((chunks * 2 * tok, LANES), BF16),
            pltpu.VMEM((ny, XL * block, LANES), BF16),
            pltpu.VMEM((ny, XL * block, LANES), BF16),
            pltpu.VMEM((XL, ny * block, LANES), BF16),
            pltpu.VMEM((nz, nt, nx, ny * block, LANES), BF16),
            pltpu.VMEM((per * size, padded), BF16),
            pltpu.VMEM((groups, ne, piece * (padded // LANES), LANES), BF16),
            pltpu.VMEM((groups, ne, piece * (padded // LANES), LANES), BF16),
            pltpu.VMEM((nr, tok, LANES), F32),
            pltpu.VMEM((groups, per * XH * 2 * tok, ne * piece), BF16),
            pltpu.VMEM((groups, per * XH * 2 * tok, 1), F32),
            pltpu.VMEM((nr, tok, padded), BF16),
            pltpu.VMEM((nr, tok, padded), BF16),
            pltpu.VMEM((tok, nr, width), BF16),
            pltpu.VMEM((per * size, per * size), BF16),
            pltpu.VMEM((steps * heads, latent_cache.shape[1]), F32),
            pltpu.VMEM((steps, heads, full - ROPE), BF16),
            dma((6,)),
            dma((8,)),
            dma,
            dma,
            dma,
            dma((nz // 2, 2)),
            dma((nz // 2, 2)),
            dma((nz, 2)),
            dma,
            dma((groups,)),
            dma,
        ],
        compiler_params=pltpu.CompilerParams(
            collective_id=0, has_side_effects=True, vmem_limit_bytes=56 * 1024 * 1024
        ),
        cost_estimate=pl.CostEstimate(flops=2_000_000_000, bytes_accessed=6_000_000, transcendentals=262144),
    )(
        cache_lengths,
        block_scales[0],
        routes.T,
        route_weights.T,
        hidden_acts,
        queries.reshape(steps, heads, full),
        latent_cache[0].T,
        stored_values[0],
    )
    expert_output = gathered.reshape(tok, nr, 1, width)
    return attended.reshape(steps, 1, heads, full - ROPE), synced.T[None], expert_output


def solution(mesh):
    sizes = (mesh.shape["replica"], mesh.shape["expert"], mesh.shape["tensor"])
    placed = (
        P(None, ("replica", "expert"), "tensor", None),
        P(("replica", "expert"), None, None),
        P(("replica", "expert")),
        P(("replica", "expert"), None, None),
        P(("replica", "expert"), None),
        P(("replica", "expert"), None),
        P("expert", ("replica", "tensor"), None),
        P("expert", None, None),
    )
    return jax.shard_map(
        functools.partial(local, sizes),
        mesh=mesh,
        in_specs=placed,
        out_specs=(
            P(None, ("replica", "expert"), "tensor", None),
            P("expert", None, ("replica", "tensor")),
            P(("replica", "expert"), None, "tensor", None),
        ),
        check_vma=False,
    )
```

```python
import functools

import jax
import jax.numpy as jnp
from jax import lax
from jax.experimental import pallas as pl
from jax.experimental.pallas import tpu as pltpu
from jax.sharding import PartitionSpec as P

XH = 2
XL = 4
SLOTS = 2
QB = 128
ROPE = 64
SCORE_SCALE = 192.0 ** (-0.5)
LANES = 128
WAVES = (7, 12, 12, 0)
PER = 4
MESH = pl.DeviceIdType.MESH
F32 = jnp.float32
BF16 = jnp.bfloat16


def iota(shape, axis):
    return lax.broadcasted_iota(jnp.int32, shape, axis)


def log2(n):
    return n.bit_length() - 1


def onehot(mask):
    return jnp.where(mask, 1.0, 0.0).astype(BF16)


def settle(ref, sem):
    pltpu.make_async_copy(ref, ref, sem).wait()


def kernel(
    sizes,
    lengths,
    scales,
    routes,
    weights,
    hidden,
    queries,
    cache,
    stored,
    attended,
    synced,
    gathered,
    pack_out,
    pack_in,
    wfull,
    stacked,
    y_out,
    y_in,
    x_out,
    rows,
    products,
    r_out,
    r_in,
    meta,
    pick,
    gains,
    f_out,
    f_in,
    final,
    perm,
    scores,
    att,
    local_sem,
    send_sem,
    w_sem,
    y_sem,
    x_sem,
    right_sem,
    left_sem,
    pair_sem,
    meta_sem,
    r_sem,
    f_sem,
):
    nr, ne, nt = sizes
    nz, ny = nr // XH, ne // XL
    nx = XH * XL
    tok = routes.shape[1]
    depth = stored.shape[0]
    width = stored.shape[1] // (nr * nt)
    chunks = hidden.shape[2] // (nt * LANES)
    half = chunks * LANES
    groups = nz // PER
    per = PER
    block = chunks * SLOTS
    line_rows = ny * SLOTS
    chunk_rows = nx * line_rows
    piece = per * XH * SLOTS
    halves = products.shape[1] // LANES
    order = [0]
    for step in range(1, nz // 2):
        order += [-step, step]
    order.append(nz // 2)

    r, e, t = lax.axis_index("replica"), lax.axis_index("expert"), lax.axis_index("tensor")
    xh, z = r // nz, r % nz
    y, xl = e // XL, e % XL
    x = xh * XL + xl
    me = r * nt + t

    def to(rep, exp, ten):
        return {"replica": rep, "expert": exp, "tensor": ten}

    def remote(src, dst, send, recv, target):
        return pltpu.make_async_remote_copy(
            src, dst, send_sem.at[send], recv, device_id=target, device_id_type=MESH
        )

    barrier = pltpu.get_barrier_semaphore()

    def greet(rep, exp, ten):
        pl.semaphore_signal(barrier, inc=1, device_id=to(rep, exp, ten), device_id_type=MESH)

    @pl.loop(1, nr * nt)
    def _(d):
        other = (me + d) % (nr * nt)
        greet(other // nt, e, other % nt)

    @pl.loop(1, ne)
    def _(d):
        greet(r, (e + d) % ne, t)

    for dh in range(1, XH):
        for dl in range(1, XL):
            greet((xh + dh) % XH * nz + z, y * XL + (xl + dl) % XL, t)

    named = routes[...].astype(F32)
    line = [named[k : k + 1, :] for k in range(2)]
    eye = iota((tok, tok), 0) == iota((tok, tok), 1)
    before = iota((tok, tok), 1) < iota((tok, tok), 0)
    column = [jnp.sum(jnp.where(eye, v, 0.0), axis=1, keepdims=True) for v in line]
    gain = [jnp.sum(jnp.where(eye, weights[k : k + 1, :], 0.0), axis=1, keepdims=True) for k in range(2)]
    slot = []
    for k in range(2):
        count = jnp.sum(jnp.where((column[k] == line[k]) & before, 1.0, 0.0), axis=1, keepdims=True)
        for other in range(k):
            count += jnp.sum(jnp.where(column[k] == line[other], 1.0, 0.0), axis=1, keepdims=True)
        slot.append(count)
    pairs = 2 * tok
    target = jnp.concatenate([column[k] * block + slot[k] for k in range(2)], axis=0)
    lane = iota((pairs, chunks * pairs), 1)
    spread = jnp.where((lane & (pairs - 1)) == iota((pairs, chunks * pairs), 0), target, 0.0)
    wanted = jnp.sum(spread, axis=0, keepdims=True)
    wanted = wanted + ((iota((1, chunks * pairs), 1) >> log2(pairs)) * SLOTS).astype(F32)
    placer = onehot(iota((ne * block, chunks * pairs), 0).astype(F32) == wanted)
    for c in range(chunks):
        start = pl.multiple_of(t * half + c * LANES, LANES)
        part = hidden[:, :, pl.ds(start, LANES)]
        for k in range(2):
            stacked[c * pairs + k * tok : c * pairs + (k + 1) * tok, :] = part[:, k, :]
    y_out[...] = (
        jnp.dot(placer, stacked[...], preferred_element_type=F32).astype(BF16).reshape(y_out.shape)
    )
    lane = iota((tok, LANES), 1)
    note = jnp.zeros((tok, LANES), F32)
    for k in range(2):
        note = jnp.where(lane == k, column[k] * piece + slot[k], note)
        note = jnp.where(lane == 2 + k, gain[k], note)
    meta[r] = note

    window = 4 * width
    tiles = window // QB
    high = width // 2

    @pl.loop(0, nr * nt // 4)
    def _(q):
        values = stored[:, pl.ds(pl.multiple_of(q * window, QB), window)].astype(F32)
        row = me * depth // QB
        values = jnp.concatenate(
            [values[:, j * QB : (j + 1) * QB] * scales[row, q * tiles + j] for j in range(tiles)], axis=1
        ).astype(BF16)
        values = values.T
        for b in range(4):
            pack_out[q * 4 + b] = jnp.concatenate(
                [values[width * b + high * g : width * b + high * (g + 1), :] for g in range(2)], axis=1
            )

    pl.semaphore_wait(barrier, nr * nt - 1 + ne - 1 + (XH - 1) * (XL - 1))

    @pl.loop(1, ny)
    def _(d):
        other = (y + d) % ny
        remote(y_out.at[other], y_in.at[y], 0, y_sem, to(r, other * XL + xl, t)).start()

    own = pltpu.make_async_copy(y_out.at[y], y_in.at[y], local_sem.at[0])
    own.start()

    def send_weights(first, end):
        @pl.loop(first, end)
        def _(d):
            other = (me + d) % (nz * nt) + (xh + d // (nz * nt)) % XH * (nz * nt)
            remote(pack_out.at[other], pack_in.at[me], 2, w_sem, to(other // nt, e, other % nt)).start()

    cuts = [1]
    for wave in WAVES:
        cuts.append(min(nr * nt, cuts[-1] + wave))
    cuts[-1] = nr * nt
    send_weights(cuts[0], cuts[1])
    mine = pltpu.make_async_copy(pack_out.at[me], pack_in.at[me], local_sem.at[1])
    mine.start()

    size = ny * block
    out_row, in_row = iota((size, 1), 0), iota((size, size), 1)
    source = (
        ((out_row >> log2(SLOTS)) & (ny - 1)) * block
        + (out_row >> log2(line_rows)) * SLOTS
        + (out_row & (SLOTS - 1))
    )
    turn = onehot(source == in_row)
    own.wait()
    settle(y_in.at[pl.ds(0, ny - 1)], y_sem)
    turned = jnp.concatenate(
        [
            jnp.concatenate([y_in[k, l * block : (l + 1) * block, :] for k in range(ny)], axis=0)
            for l in range(XL)
        ],
        axis=1,
    )
    turned = jnp.dot(turn, turned, preferred_element_type=F32).astype(BF16)
    for l in range(XL):
        x_out[l] = turned[:, l * LANES : (l + 1) * LANES]

    @pl.loop(1, nx)
    def _(d):
        other = (x + d) % nx
        target = to(other // XL * nz + z, y * XL + other % XL, t)
        remote(x_out.at[other % XL], rows.at[z, t, x], 3, x_sem, target).start()

    kept = pltpu.make_async_copy(x_out.at[xl], rows.at[z, t, x], local_sem.at[2])
    kept.start()
    send_weights(cuts[1], cuts[2])

    @pl.loop(1, nr)
    def _(d):
        other = (r + d) % nr
        remote(meta.at[r], meta.at[r], 1, meta_sem, to(other, e, t)).start()

    steps, heads, full = queries.shape
    positions = cache.shape[1]

    def score():
        scores[...] = jnp.dot(
            queries[...].reshape(steps * heads, full), cache[...], preferred_element_type=F32
        )

    def attend(s):
        position = iota((1, positions), 1)
        seen = jnp.where(
            position < lengths[0] + s + 1, scores[s * heads : (s + 1) * heads] * SCORE_SCALE, -jnp.inf
        )
        raised = jnp.exp(seen - jnp.max(seen, axis=-1, keepdims=True))
        shares = raised * (1.0 / jnp.sum(raised, axis=-1, keepdims=True))
        att[s] = lax.dot_general(
            shares.astype(BF16), cache[: full - ROPE, :], (((1,), (1,)), ((), ())),
            preferred_element_type=F32,
        ).astype(BF16)

    def permute():
        size = per * chunk_rows
        out_row, in_row = iota((size, 1), 0), iota((size, size), 1)
        home, rest = out_row >> log2(piece), out_row & (piece - 1)
        source = (
            (rest >> log2(XH * SLOTS)) * chunk_rows
            + (((rest >> log2(SLOTS)) & (XH - 1)) * XL + (home & (XL - 1))) * line_rows
            + (home >> log2(XL)) * SLOTS
            + (rest & (SLOTS - 1))
        )
        perm[...] = onehot(source == in_row)

    def homes(group):
        for index in range(group * per, (group + 1) * per):
            for h in range(XH):
                yield index - group * per, h, h * nz + (z + order[index] + nz) % nz

    def prepare(group):
        position = iota((tok, ne * piece), 1).astype(F32)
        for index, h, home in homes(group):
            facts = meta[home]
            for k in range(2):
                start = ((index * XH + h) * 2 + k) * tok
                place = facts[:, k : k + 1] + (index * XH + h) * SLOTS
                pick[group, start : start + tok, :] = onehot(position == place)
                gains[group, start : start + tok, :] = facts[:, 2 + k : 3 + k]

    hx = nx // 2

    def piece_of(offset, h):
        return rows.at[(z + offset + nz) % nz, t, pl.ds(h * hx, hx)]

    def ring(offset, h, sem, direction):
        target = to(xh * nz + (z + direction + nz) % nz, e, t)
        return remote(piece_of(offset, h), piece_of(offset, h), 4, sem, target)

    def pair(index, h):
        ref = piece_of(order[index], h)
        return remote(ref, ref, 5, pair_sem.at[index, h], to(r, e, 1 - t))

    def product(first, end):
        for index in range(first, end):
            for h in range(2):
                pair(index, h).wait_recv()
        lefts = []
        for index in range(first, end):
            chunk = rows.at[(z + order[index] + nz) % nz]
            lefts.append(
                jnp.concatenate(
                    [
                        chunk[u, :, c * line_rows : (c + 1) * line_rows, :].reshape(chunk_rows, LANES)
                        for u in range(nt)
                        for c in range(chunks)
                    ],
                    axis=1,
                )
            )
        value = lax.dot_general(
            jnp.concatenate(lefts, axis=0), wfull[...], (((1,), (1,)), ((), ())),
            preferred_element_type=F32,
        ).astype(BF16)
        where = first % per * chunk_rows
        products[where : where + (end - first) * chunk_rows, :width] = value

    def unpack():
        mine.wait()
        settle(pack_in.at[pl.ds(0, nr * nt - 1)], w_sem)

        @pl.loop(0, nr)
        def _(s):
            values = [pack_in[s * nt + u] for u in range(nt)]
            for g in range(2):
                wfull[high * g : high * (g + 1), pl.ds(pl.multiple_of(s * nt * depth, nt * depth), nt * depth)] = (
                    jnp.concatenate([v[:, depth * g : depth * (g + 1)] for v in values], axis=1)
                )

    def send_back(group):
        value = jnp.dot(perm[...], products[...], preferred_element_type=F32).astype(BF16)
        for g in range(halves):
            r_out[group, :, g * piece : (g + 1) * piece, :] = value[:, g * LANES : (g + 1) * LANES].reshape(
                ne, piece, LANES
            )

        @pl.loop(1, ne)
        def _(d):
            other = (e + d) % ne
            remote(r_out.at[group, other], r_in.at[group, e], 6, r_sem.at[group], to(r, other, t)).start()

        here = pltpu.make_async_copy(r_out.at[group, e], r_in.at[group, e], local_sem.at[5])
        here.start()
        here.wait()

    def combine(group):
        settle(r_in.at[group, pl.ds(0, ne - 1)], r_sem.at[group])
        arrived = r_in[group]
        arrived = jnp.concatenate(
            [arrived[:, g * piece : (g + 1) * piece, :].reshape(ne * piece, LANES) for g in range(halves)], axis=1
        )
        picked = jnp.dot(pick[group], arrived, preferred_element_type=F32) * gains[group]
        for index, h, home in homes(group):
            start = (index * XH + h) * 2 * tok
            f_out[home] = (picked[start : start + tok] + picked[start + tok : start + 2 * tok]).astype(BF16)
        for index, h, home in homes(group):
            if group == 0 and index == 0:
                @pl.when(h == xh)
                def _():
                    f_in[home] = f_out[home]

                @pl.when(h != xh)
                def _():
                    remote(f_out.at[home], f_in.at[r], 7, f_sem, to(home, e, t)).start()
            else:
                remote(f_out.at[home], f_in.at[r], 7, f_sem, to(home, e, t)).start()

    last = nz // 2

    def when(index):
        return min(last, max(2, (index + 1) // 2))

    def forward(step):
        for h in range(2):
            if step == 0:
                ring(0, h, right_sem.at[0, h], 1).start()
                ring(0, h, left_sem.at[0, h], -1).start()
                pair(0, h).start()
                continue
            if step < last or h == 0:
                ring(-step, h, right_sem.at[step - 1, h], 1).wait_recv()
                if step + 1 < last or (step + 1 == last and h == 0):
                    ring(-step, h, right_sem.at[step, h], 1).start()
                pair(2 * step - 1, h).start()
            if step < last or h == 1:
                ring(step, h, left_sem.at[step - 1, h], -1).wait_recv()
                if step + 1 < last or (step + 1 == last and h == 1):
                    ring(step, h, left_sem.at[step, h], -1).start()
                pair(2 * step if step < last else 2 * step - 1, h).start()

    score()
    kept.wait()
    settle(rows.at[0, 0, pl.ds(0, nx - 1)], x_sem)
    forward(0)
    send_weights(cuts[2], cuts[3])
    for s in range(steps):
        attend(s)
    attended_copy = pltpu.make_async_copy(att, attended, local_sem.at[3])
    attended_copy.start()
    permute()
    settle(meta.at[pl.ds(0, nr - 1)], meta_sem)
    for group in range(groups):
        prepare(group)
    products[...] = jnp.zeros_like(products)
    early = 0
    for step in range(1, last + 1):
        forward(step)
        if step == 1:
            send_weights(cuts[3], cuts[4])
        if step == min(2, last):
            unpack()
            synced_copy = pltpu.make_async_copy(wfull, synced, local_sem.at[4])
            synced_copy.start()
        for group in range(groups):
            first, end = group * per, (group + 1) * per
            if step == when(end - 1):
                if first < end - 1 and step > when(end - 2):
                    product(end - 1, end)
                else:
                    product(first, end)
                send_back(group)
            elif step == when(end - 2):
                product(first, end - 1)
        if step == last - 1 and groups > 1 and when(per - 1) <= step:
            combine(0)
            early = 1
    for group in range(early, groups):
        combine(group)

    settle(y_out.at[pl.ds(0, ny - 1)], send_sem.at[0])
    settle(meta.at[pl.ds(0, nr - 1)], send_sem.at[1])
    settle(pack_out.at[pl.ds(0, nr * nt - 1)], send_sem.at[2])
    settle(rows.at[0, 0, pl.ds(0, nx - 1)], send_sem.at[3])
    settle(rows.at[pl.ds(0, nz - 1), 0], send_sem.at[4])
    settle(rows.at[:, 0], send_sem.at[5])
    for group in range(groups):
        settle(r_out.at[group, pl.ds(0, ne - 1)], send_sem.at[6])
    settle(f_out.at[pl.ds(0, nr - 1)], send_sem.at[7])
    attended_copy.wait()
    synced_copy.wait()
    settle(f_in.at[pl.ds(0, nr - 1)], f_sem)
    size = nr * tok
    out_row, in_row = iota((size, 1), 0), iota((size, size), 1)
    source = (out_row & (nr - 1)) * tok + (out_row >> log2(nr))
    value = jnp.dot(
        onehot(source == in_row), f_in[...].reshape(size, f_in.shape[2]), preferred_element_type=F32
    )
    final[...] = value[:, :width].astype(BF16).reshape(tok, nr, width)
    result = pltpu.make_async_copy(final, gathered, local_sem.at[1])
    result.start()
    result.wait()


def write_results(a, b, c, a_out, b_out, c_out, sem):
    parts = 4
    rows = b.shape[0] // parts
    copies = [pltpu.make_async_copy(a, a_out, sem.at[0]), pltpu.make_async_copy(c, c_out, sem.at[1])]
    for k in range(parts):
        copies.append(
            pltpu.make_async_copy(b.at[pl.ds(k * rows, rows)], b_out.at[pl.ds(k * rows, rows)], sem.at[2 + k])
        )
    for copy in copies:
        copy.start()
    for copy in copies:
        copy.wait()


def local(sizes, queries, latent_cache, cache_lengths, hidden_acts, routes, route_weights, stored_values, block_scales):
    nr, ne, nt = sizes
    nz, ny, nx = nr // XH, ne // XL, XH * XL
    steps, _, heads, full = queries.shape
    tok, _, ffn = hidden_acts.shape
    depth, columns = stored_values.shape[1:]
    width = columns // (nr * nt)
    padded = -(-width // LANES) * LANES
    chunks = ffn // (nt * LANES)
    block = chunks * SLOTS
    groups = nz // PER
    per = PER
    piece = per * XH * SLOTS
    size = nx * ny * SLOTS
    vmem = pl.BlockSpec(memory_space=pltpu.VMEM)
    smem = pl.BlockSpec(memory_space=pltpu.SMEM)
    hbm = pl.BlockSpec(memory_space=pl.ANY)
    dma = pltpu.SemaphoreType.DMA
    attended, synced, gathered = pl.pallas_call(
        functools.partial(kernel, sizes),
        out_shape=[
            jax.ShapeDtypeStruct((steps, heads, full - ROPE), BF16),
            jax.ShapeDtypeStruct((width, ffn), BF16),
            jax.ShapeDtypeStruct((tok, nr, width), BF16),
        ],
        in_specs=[smem, smem, vmem, vmem, vmem, vmem, vmem, vmem],
        out_specs=[hbm, hbm, hbm],
        scratch_shapes=[
            pltpu.VMEM((nr * nt, width // 2, 2 * depth), BF16),
            pltpu.VMEM((nr * nt, width // 2, 2 * depth), BF16),
            pltpu.VMEM((width, ffn), BF16),
            pltpu.VMEM((chunks * 2 * tok, LANES), BF16),
            pltpu.VMEM((ny, XL * block, LANES), BF16),
            pltpu.VMEM((ny, XL * block, LANES), BF16),
            pltpu.VMEM((XL, ny * block, LANES), BF16),
            pltpu.VMEM((nz, nt, nx, ny * block, LANES), BF16),
            pltpu.VMEM((per * size, padded), BF16),
            pltpu.VMEM((groups, ne, piece * (padded // LANES), LANES), BF16),
            pltpu.VMEM((groups, ne, piece * (padded // LANES), LANES), BF16),
            pltpu.VMEM((nr, tok, LANES), F32),
            pltpu.VMEM((groups, per * XH * 2 * tok, ne * piece), BF16),
            pltpu.VMEM((groups, per * XH * 2 * tok, 1), F32),
            pltpu.VMEM((nr, tok, padded), BF16),
            pltpu.VMEM((nr, tok, padded), BF16),
            pltpu.VMEM((tok, nr, width), BF16),
            pltpu.VMEM((per * size, per * size), BF16),
            pltpu.VMEM((steps * heads, latent_cache.shape[1]), F32),
            pltpu.VMEM((steps, heads, full - ROPE), BF16),
            dma((6,)),
            dma((8,)),
            dma,
            dma,
            dma,
            dma((nz // 2, 2)),
            dma((nz // 2, 2)),
            dma((nz, 2)),
            dma,
            dma((groups,)),
            dma,
        ],
        compiler_params=pltpu.CompilerParams(
            collective_id=0, has_side_effects=True, vmem_limit_bytes=56 * 1024 * 1024
        ),
        cost_estimate=pl.CostEstimate(flops=2_000_000_000, bytes_accessed=6_000_000, transcendentals=262144),
    )(
        cache_lengths,
        block_scales[0],
        routes.T,
        route_weights.T,
        hidden_acts,
        queries.reshape(steps, heads, full),
        latent_cache[0].T,
        stored_values[0],
    )
    results = [attended, synced, gathered]
    attended, synced, gathered = pl.pallas_call(
        write_results,
        out_shape=[jax.ShapeDtypeStruct(v.shape, v.dtype) for v in results],
        in_specs=[hbm] * 3,
        out_specs=[hbm] * 3,
        scratch_shapes=[dma((6,))],
    )(*results)
    expert_output = gathered.reshape(tok, nr, 1, width)
    return attended.reshape(steps, 1, heads, full - ROPE), synced.T[None], expert_output


def solution(mesh):
    sizes = (mesh.shape["replica"], mesh.shape["expert"], mesh.shape["tensor"])
    placed = (
        P(None, ("replica", "expert"), "tensor", None),
        P(("replica", "expert"), None, None),
        P(("replica", "expert")),
        P(("replica", "expert"), None, None),
        P(("replica", "expert"), None),
        P(("replica", "expert"), None),
        P("expert", ("replica", "tensor"), None),
        P("expert", None, None),
    )
    return jax.shard_map(
        functools.partial(local, sizes),
        mesh=mesh,
        in_specs=placed,
        out_specs=(
            P(None, ("replica", "expert"), "tensor", None),
            P("expert", None, ("replica", "tensor")),
            P(("replica", "expert"), None, "tensor", None),
        ),
        check_vma=False,
    )
```
